128 devices in a mesh: section: 16 (over z, y), dp: 8 (over x, core).
Axes of the slice: x: 4, y: 4, z: 4, core: 2. Of those that a mesh axis runs over, the one named last changes fastest.
Arguments:
- acts: bfloat16 [16, 3, 384, 8192], P('section', None, 'dp'), may hold values from -6 to 6
- out_grad: bfloat16 [3, 384, 8192], P(None, 'dp'), may hold values from -6 to 6
- w_value: bfloat16 [16, 8192, 512], P('section', 'dp'), may hold values from -0.0625 to 0.0625
- w_output: bfloat16 [16, 512, 8192], P('section', None, 'dp'), may hold values from -0.109375 to 0.109375
- order: int32 [8, 3], P('dp'), may hold values from 0 to 2, each once within a row
- alive: int32 [8], replicated, may hold values from 0 to 1, as said below
- flags: int32 [16, 8], P('section', 'dp'), may hold values 0 or 1
- clip_rms: float32 [1], replicated, may hold values from 0.1 to 0.5
- master: float32 [16, 8192, 1024], P('section', 'dp'), may hold values from -3 to 3
- moment_one: bfloat16 [16, 8192, 1024], P('section', 'dp'), may hold values from -2 to 2
- moment_two: bfloat16 [16, 8192, 1024], P('section', 'dp'), may hold values from 0.0099487305 to 0.5
Outputs:
- new_master: float32 [16, 8192, 1024], P('section', 'dp')
- new_moment_one: bfloat16 [16, 8192, 1024], P('section', 'dp')
- new_moment_two: bfloat16 [16, 8192, 1024], P('section', 'dp')
The draws below stay inside these ranges and needn't reach their ends.
Inputs may be any that keep to these rules, and one draw needn't show every extreme that they name: Each row of order names each of the 3 micro-batches once. `alive`: 1 marks a surviving replica; at least one replica survives and at least one is lost. `flags`: 1 marks an overflow.
All inputs are finite; a program needn't handle non-finite values. No bound on the sum of `flags` on one device may be relied on, other than what follows from the above.
Results may differ from the reference program's by a relative error of at most 0.009.
Values may be sent and summed in bfloat16 or wider, within the bound.
No kernel may reach another device: no remote copies, remote signals or barrier semaphores. Data moves between devices by JAX's collectives and lax.ppermute only.
A program may use at most 128 MiB of HBM per device.

```python
import math
import jax
import jax.numpy as jnp
from jax import lax

D = 8192
TOK = 48
MICRO = 3
HW = 512
SECTIONS = 16
REPLICAS = 8
TOKENS = 384


def draw_alive(key, part):
    key = jax.random.fold_in(key, 7)
    pattern = jax.random.randint(key, (), 1, 2 ** REPLICAS - 1, dtype=jnp.int32)
    powers = 2 ** jnp.arange(REPLICAS, dtype=jnp.int32)
    return (pattern // powers % 2).astype(jnp.int32)


def with_ends(drawn, own_key, least, top_value):
    extent = drawn.shape
    place = [jax.random.randint(jax.random.fold_in(own_key, axis), (), 0, extent[axis]) for axis in range(len(extent))]
    drawn = drawn.at[tuple(place)].set(least)
    longest = extent.index(max(extent))
    place[longest] = (place[longest] + 1) % extent[longest]
    return drawn.at[tuple(place)].set(top_value)


def level_of(key, dims, cuts, smallest, largest):
    gain = 1.0
    for axis_at, shards_of in cuts:
        heights = jax.random.uniform(jax.random.fold_in(jax.random.fold_in(key, 6), axis_at), (shards_of,), jnp.float32, smallest / len(cuts), largest / len(cuts))
        gain = gain * jnp.repeat(jnp.exp(heights), dims[axis_at] // shards_of).reshape((-1,) + (1,) * (len(dims) - 1 - axis_at))
    return gain


def centred(own_key, extent, scale, reach, split=(), kind=jnp.bfloat16):
    loudness = level_of(own_key, extent, split, -0.22, 0.18) if split else 1.0
    result = jax.random.normal(own_key, extent, jnp.float32) * scale * loudness
    return jnp.minimum(jnp.maximum(result, -reach), reach).astype(kind)


def setup_inputs(seed: int = 0) -> dict:
    keys = jax.random.split(jax.random.key(seed), 12)
    acts = centred(keys[0], (SECTIONS, MICRO, TOKENS, D), 1.0, 6.0, ((0, 16), (2, 8)))
    out_grad = centred(keys[1], (MICRO, TOKENS, D), 1.0, 6.0, ((1, 8),))
    w_value = centred(keys[2], (SECTIONS, D, HW), D ** -0.5, 0.0625, ((0, 16), (1, 8)))
    w_output = centred(keys[3], (SECTIONS, HW, D), (HW * SECTIONS // 3) ** -0.5, 0.109375, ((0, 16), (2, 8)))
    order = jax.vmap(lambda own: jax.random.permutation(own, MICRO))(jax.random.split(keys[4], REPLICAS)).reshape((REPLICAS, MICRO)).astype(jnp.int32)
    alive = draw_alive(jax.random.fold_in(keys[11], 71), 0)
    flags = with_ends((jax.random.randint(keys[6], (SECTIONS, REPLICAS), 0, 16) < 1).astype(jnp.int32), jax.random.fold_in(keys[6], 1), 0, 1)
    clip_rms = jnp.clip(jnp.exp(jax.random.uniform(keys[7], (1,), jnp.float32, math.log(0.1), math.log(0.5))), 0.1, 0.5)
    master = centred(keys[8], (SECTIONS, D, 2 * HW), 0.5, 3.0, ((0, 16), (1, 8)), jnp.float32)
    moment_one = centred(keys[9], (SECTIONS, D, 2 * HW), 0.3, 2.0, ((0, 16), (1, 8)))
    moment_two = jnp.clip(jnp.exp(math.log(0.5) - 3.9171631 * jax.random.uniform(keys[10], (SECTIONS, D, 2 * HW), jnp.float32) ** level_of(keys[10], (SECTIONS, D, 2 * HW), ((0, 16), (1, 8)), -0.2, 0.2)), 0.0099487305, 0.5).astype(jnp.bfloat16)
    return {"acts": acts, "out_grad": out_grad, "w_value": w_value, "w_output": w_output, "order": order, "alive": alive, "flags": flags, "clip_rms": clip_rms, "master": master, "moment_one": moment_one, "moment_two": moment_two}


beta_one = 0.9
beta_two = 0.95
adam_eps = 1e-08
learn_rate = 0.01
weight_decay = 0.1
step_count = 100

def section_terms(picked, gradient, value_weight, output_weight):
    picked_f = picked.astype(jnp.float32)
    grad_f = gradient.astype(jnp.float32)
    value_f = value_weight.astype(jnp.float32)
    output_f = output_weight.astype(jnp.float32)
    hidden = jnp.einsum('mrtd,dh->mrth', picked_f, value_f).astype(jnp.bfloat16)
    back = jnp.einsum('mrtd,hd->mrth', grad_f, output_f).astype(jnp.bfloat16)
    back_f = back.astype(jnp.float32)
    lower = (grad_f + jnp.einsum('mrth,dh->mrtd', back_f, value_f)).astype(jnp.bfloat16)
    value_part = jnp.einsum('mrtd,mrth->rdh', picked_f, back_f)
    output_part = jnp.einsum('mrtd,mrth->rdh', grad_f, hidden.astype(jnp.float32))
    terms = jnp.concatenate([value_part, output_part], axis=2).astype(jnp.bfloat16)
    terms = lax.optimization_barrier(terms).astype(jnp.float32)
    return (lower, terms)

def reference(acts, out_grad, w_value, w_output, order, alive, flags, clip_rms, master, moment_one, moment_two):
    keep = alive[None, :] * (1 - flags)
    counts = jnp.maximum(lax.optimization_barrier(jnp.sum(keep, axis=1)), 1).astype(jnp.float32)
    keep_f = keep.astype(jnp.float32)
    gradient = out_grad.reshape(MICRO, REPLICAS, TOK, D)
    collected = []
    for section in range(SECTIONS - 1, -1, -1):
        stash = acts[section].reshape(MICRO, REPLICAS, TOK, D)
        picked = jnp.stack([jnp.take(stash[:, replica], order[replica], axis=0) for replica in range(REPLICAS)], axis=1)
        gradient, terms = section_terms(picked, gradient, w_value[section], w_output[section])
        collected.append(jnp.einsum('r,rdh->dh', keep_f[section], terms) / counts[section])
    grads = jnp.stack(collected[::-1])
    norm = jnp.sqrt(jnp.sum(grads * grads))
    threshold = clip_rms[0] * jnp.sqrt(jnp.float32(2 * D * HW * SECTIONS))
    factor = jnp.minimum(1.0, threshold / (norm + 1e-06))
    scaled = factor * grads
    new_one = beta_one * moment_one.astype(jnp.float32) + (1.0 - beta_one) * scaled
    new_two = beta_two * moment_two.astype(jnp.float32) + (1.0 - beta_two) * scaled * scaled
    hat_one = new_one / (1.0 - beta_one ** step_count)
    hat_two = new_two / (1.0 - beta_two ** step_count)
    new_master = master - learn_rate * (hat_one / (jnp.sqrt(hat_two) + adam_eps) + weight_decay * master)
    return (new_master, new_one.astype(jnp.bfloat16), new_two.astype(jnp.bfloat16))
```

```python
import math

import jax
import jax.numpy as jnp
from jax import lax
from jax.sharding import Mesh
from jax.sharding import PartitionSpec as P

beta_one = 0.9
beta_two = 0.95
adam_eps = 1e-08
learn_rate = 0.01
weight_decay = 0.1
step_count = 100

SECTION = ("z", "y")
DP = ("x", "core")
PLANE = ("y", "core")


def dot(left, right, dims):
    return lax.dot_general(left, right, (dims, ((), ())), preferred_element_type=jnp.float32)


def swap(value, axis, mask):
    return lax.ppermute(value, axis, [(i, i ^ mask) for i in range(lax.axis_size(axis))])


def sum_over_x(part):
    part = part.astype(jnp.bfloat16)
    rows = part.shape[0] // 2
    halves = (part[:rows], part[rows:])
    masks = ((1, 3), (3, 1))
    for turn in range(2):
        got = [swap(half, "x", masks[i][turn]) for i, half in enumerate(halves)]
        halves = [
            (half.astype(jnp.float32) + other.astype(jnp.float32)).astype(jnp.bfloat16)
            for half, other in zip(halves, got)
        ]
    return jnp.concatenate(halves, axis=0)


def sum_over_all(value):
    for axis, masks in (("core", (1,)), ("x", (1, 3)), ("y", (1, 3)), ("z", (1, 3))):
        for mask in masks:
            value = value + swap(value, axis, mask)
    return value


def shards(
    acts, out_grad, w_value, w_output, order, alive, flags, clip_rms, master, moment_one, moment_two
):
    z, y, x, core = (lax.axis_index(axis) for axis in ("z", "y", "x", "core"))
    planes, columns, across = (lax.axis_size(axis) for axis in ("z", "y", "x"))
    replicas = across * lax.axis_size("core")
    own_value, own_output = w_value[0], w_output[0]
    share, head_size = own_value.shape
    micro, tok_rows, width = out_grad.shape
    rows = micro * tok_rows
    chip_width = 2 * share

    output_weight = lax.all_gather(own_output, PLANE, axis=0)
    value_weight = lax.all_gather(own_value, PLANE, axis=0)
    flag_row = lax.all_gather(flags[0, 0], DP)

    top = out_grad.reshape(rows, width)
    own_slice = lax.dynamic_slice(top, (0, x * chip_width), (rows, chip_width))
    gradient = jnp.where(jnp.logical_and(z == planes - 1, x == y), own_slice, jnp.zeros_like(own_slice))
    for turn in range(1, across):
        other = lax.rem(x + turn, across)
        piece = lax.dynamic_slice(top, (0, other * chip_width), (rows, chip_width))
        base = (planes - 1) * columns * across
        pairs = [
            (base + i * across + i, base + i * across + (i + turn) % across) for i in range(columns)
        ]
        gradient = gradient + lax.ppermute(piece, ("z", "y", "x"), pairs)

    keep = alive * (1 - flag_row)
    replica = lax.axis_index(DP)
    own_keep = (alive[replica] * (1 - flags[0, 0])).astype(jnp.bfloat16)
    picked = jnp.take(acts[0], order[0], axis=0).reshape(rows, width) * own_keep
    picked = lax.all_to_all(picked, DP, split_axis=1, concat_axis=0, tiled=True)
    hidden_part = dot(picked, own_value, ((1,), (0,))).astype(jnp.bfloat16)
    hidden_part = lax.all_to_all(
        hidden_part.reshape(replicas, rows, head_size), DP, split_axis=0, concat_axis=0, tiled=True
    )
    hidden = jnp.sum(hidden_part.astype(jnp.float32), axis=0).astype(jnp.bfloat16)
    hidden = lax.all_gather(hidden, DP, axis=0, tiled=True)

    kept_gradient = jnp.zeros((rows, chip_width), jnp.bfloat16)
    kept_back = [jnp.zeros((rows, head_size), jnp.bfloat16) for _ in range(columns)]
    for turn in range(planes):
        kept_gradient = kept_gradient + gradient
        for at in reversed(range(columns)):
            part = dot(gradient[:, :share], output_weight[2 * at], ((1,), (1,))) + dot(
                gradient[:, share:], output_weight[2 * at + 1], ((1,), (1,))
            )
            back = sum_over_x(part)
            kept_back[at] = kept_back[at] + back
            if turn < planes - 1 or at > 0:
                weight = value_weight[2 * at : 2 * at + 2].reshape(chip_width, head_size)
                gradient = (gradient.astype(jnp.float32) + dot(back, weight, ((1,), (1,)))).astype(
                    jnp.bfloat16
                )
        if turn < planes - 1:
            gradient = lax.ppermute(gradient, "z", [(i, i - 1) for i in range(1, planes)])

    gradients = [None] * columns
    gradient = kept_gradient
    for at in reversed(range(columns)):
        gradients[at] = gradient
        if at > 0:
            weight = value_weight[2 * at : 2 * at + 2].reshape(chip_width, head_size)
            gradient = (
                gradient.astype(jnp.float32) + dot(kept_back[at], weight, ((1,), (1,)))
            ).astype(jnp.bfloat16)
    sent = jnp.stack(
        [piece[:, half * share : (half + 1) * share] for piece in gradients for half in range(2)]
    )
    grad_rows = lax.all_to_all(sent, PLANE, split_axis=0, concat_axis=0, tiled=True)
    grad_rows = grad_rows.reshape(replicas * rows, share)
    backs = lax.all_to_all(jnp.stack(kept_back), "y", split_axis=0, concat_axis=0, tiled=True)
    others = swap(backs, "core", 1)
    back_rows = jnp.stack(
        [jnp.where(core == 0, backs, others), jnp.where(core == 0, others, backs)], axis=1
    ).reshape(replicas * rows, head_size)

    value_part = dot(picked, back_rows, ((0,), (0,)))
    output_part = dot(grad_rows, hidden, ((0,), (0,)))
    contributors = jnp.maximum(jnp.sum(keep).astype(jnp.float32), 1.0)
    grad_share = jnp.concatenate([value_part, output_part], axis=1) / contributors
    total_square = sum_over_all(jnp.full((8, 128), jnp.sum(grad_share * grad_share)))[0, 0]
    norm = jnp.sqrt(total_square)
    sections = planes * columns
    threshold = clip_rms[0] * math.sqrt(2 * width * head_size * sections)
    factor = jnp.minimum(1.0, threshold / (norm + 1e-06))
    scaled = factor * grad_share
    new_one = beta_one * moment_one[0].astype(jnp.float32) + (1.0 - beta_one) * scaled
    new_two = beta_two * moment_two[0].astype(jnp.float32) + (1.0 - beta_two) * scaled * scaled
    hat_one = new_one / (1.0 - beta_one**step_count)
    hat_two = new_two / (1.0 - beta_two**step_count)
    old_master = master[0]
    new_master = old_master - learn_rate * (
        hat_one / (jnp.sqrt(hat_two) + adam_eps) + weight_decay * old_master
    )
    return (
        new_master[None],
        new_one.astype(jnp.bfloat16)[None],
        new_two.astype(jnp.bfloat16)[None],
    )


def solution(mesh):
    physical = Mesh(mesh.devices.reshape(4, 4, 4, 2), ("z", "y", "x", "core"))
    in_specs = (
        P(SECTION, None, DP, None),
        P(None, DP, None),
        P(SECTION, DP, None),
        P(SECTION, None, DP),
        P(DP, None),
        P(),
        P(SECTION, DP),
        P(),
        P(SECTION, DP, None),
        P(SECTION, DP, None),
        P(SECTION, DP, None),
    )
    out_specs = (P(SECTION, DP, None), P(SECTION, DP, None), P(SECTION, DP, None))
    return jax.shard_map(
        shards, mesh=physical, in_specs=in_specs, out_specs=out_specs, check_vma=False
    )
```

```python
import math

import jax
import jax.numpy as jnp
from jax import lax
from jax.experimental import pallas as pl
from jax.experimental.pallas import tpu as pltpu
from jax.sharding import Mesh
from jax.sharding import PartitionSpec as P

beta_one = 0.9
beta_two = 0.95
adam_eps = 1e-08
learn_rate = 0.01
weight_decay = 0.1
step_count = 100

SECTION = ("z", "y")
DP = ("x", "core")
PLANE = ("y", "core")


VMEM_LIMIT = 40 * 1024 * 1024
PAIRS = ((0, 1), (0, 2), (0, 3), (1, 2), (1, 3), (2, 3))


def dot(left, right, dims):
    return lax.dot_general(left, right, (dims, ((), ())), preferred_element_type=jnp.float32)


def dot_nt(left, right):
    return dot(left, right, ((1,), (1,)))


def call(kernel, grid, in_specs, out_specs, out_shape, scratch=(), cost=None):
    return pl.pallas_call(
        kernel,
        grid=grid,
        in_specs=in_specs,
        out_specs=out_specs,
        out_shape=out_shape,
        scratch_shapes=list(scratch),
        cost_estimate=cost,
        compiler_params=pltpu.CompilerParams(vmem_limit_bytes=VMEM_LIMIT),
    )


def whole(shape):
    return pl.BlockSpec(shape, lambda *_: (0,) * len(shape))


def swap(value, axis, mask):
    return lax.ppermute(value, axis, [(i, i ^ mask) for i in range(lax.axis_size(axis))])


def turn_by(value, axis, steps):
    count = lax.axis_size(axis)
    return lax.ppermute(value, axis, [(i, (i + steps) % count) for i in range(count)])


def addends_over_x(parts, masks=((1, 3), (3, 1))):
    pairs = []
    firsts = [swap(part, "x", masks[i][0]) for i, part in enumerate(parts)]
    halves = [
        (part.astype(jnp.float32) + other.astype(jnp.float32)).astype(jnp.bfloat16)
        for part, other in zip(parts, firsts)
    ]
    for i, half in enumerate(halves):
        pairs.append((half, swap(half, "x", masks[i][1])))
    return pairs


def sum_over_all(value):
    value = value + swap(value, "core", 1)
    for axis in ("x", "y", "z"):
        got = [turn_by(value, axis, steps) for steps in (1, 3, 2)]
        value = value + got[0] + got[1] + got[2]
    return value


def project(gradient, weights, first):
    rows, chip_width = gradient.shape
    _, head_size, share = weights.shape

    def kernel(g_ref, w_ref, out_ref):
        part = dot_nt(g_ref[:, :share], w_ref[0]) + dot_nt(g_ref[:, share:], w_ref[1])
        out_ref[...] = part.astype(jnp.bfloat16)

    return call(
        kernel,
        (2,),
        [
            whole((rows, chip_width)),
            pl.BlockSpec((2, head_size, share), lambda i: (first + i, 0, 0)),
        ],
        pl.BlockSpec((rows, head_size), lambda i: (0, i)),
        jax.ShapeDtypeStruct((rows, 2 * head_size), jnp.bfloat16),
        cost=pl.CostEstimate(
            flops=4 * rows * chip_width * head_size,
            bytes_accessed=4 * chip_width * head_size,
            transcendentals=0,
        ),
    )(gradient, weights)


def solve(addends, links, b_ref):
    low, low_got, high, high_got = addends
    head_size = links.shape[-1]
    sums = []
    for own, got in ((low, low_got), (high, high_got)):
        both = own[...].astype(jnp.float32) + got[...].astype(jnp.float32)
        sums += [both[:, :head_size], both[:, head_size:]]
    backs = [None] * 4
    for at in (3, 2, 1, 0):
        total = sums[at]
        for other in range(at + 1, 4):
            link = links[:, PAIRS.index((at, other))].reshape(head_size, head_size)
            total = total + dot_nt(backs[other], link)
        backs[at] = total.astype(jnp.bfloat16)
        b_ref[at] = backs[at]


def advance(gradient, addends, links, weights):
    rows, chip_width = gradient.shape
    count, share, head_size = weights.shape
    steps = 4
    block = chip_width // steps
    weights = weights.reshape(4, steps, block, head_size)
    flat = [array for pair in addends for array in pair]

    def kernel(g_ref, low, low_got, high, high_got, m_ref, w_ref, b_ref, out_ref):
        @pl.when(pl.program_id(0) == 0)
        def _():
            solve((low, low_got, high, high_got), m_ref, b_ref)

        total = g_ref[...].astype(jnp.float32)
        for at in range(4):
            total = total + dot_nt(b_ref[at], w_ref[at, 0])
        out_ref[...] = total.astype(jnp.bfloat16)

    return call(
        kernel,
        (steps,),
        [pl.BlockSpec((rows, block), lambda i: (0, i))]
        + [whole((rows, 2 * head_size))] * 4
        + [
            whole(links.shape),
            pl.BlockSpec((4, 1, block, head_size), lambda i: (0, i, 0, 0)),
        ],
        [
            whole((4, rows, head_size)),
            pl.BlockSpec((rows, block), lambda i: (0, i)),
        ],
        [
            jax.ShapeDtypeStruct((4, rows, head_size), jnp.bfloat16),
            jax.ShapeDtypeStruct((rows, chip_width), jnp.bfloat16),
        ],
        cost=pl.CostEstimate(
            flops=2 * rows * head_size * (6 * head_size + 4 * chip_width),
            bytes_accessed=8 * chip_width * head_size + 12 * head_size * head_size,
            transcendentals=0,
        ),
    )(gradient, *flat, links, weights)


def solve_last(addends, links):
    rows, two = addends[0][0].shape
    head_size = two // 2
    flat = [array for pair in addends for array in pair]

    def kernel(low, low_got, high, high_got, m_ref, b_ref):
        solve((low, low_got, high, high_got), m_ref, b_ref)

    return call(
        kernel,
        (1,),
        [whole((rows, two))] * 4 + [whole(links.shape)],
        whole((4, rows, head_size)),
        jax.ShapeDtypeStruct((4, rows, head_size), jnp.bfloat16),
        cost=pl.CostEstimate(
            flops=12 * rows * head_size * head_size,
            bytes_accessed=12 * head_size * head_size,
            transcendentals=0,
        ),
    )(*flat, links)


def rebuild(gradient, backs, weights):
    rows, chip_width = gradient.shape
    count, share, head_size = weights.shape
    steps = 4
    block = chip_width // steps
    weights = weights.reshape(4, steps, block, head_size)

    def kernel(g_ref, b_ref, w_ref, out_ref):
        total = g_ref[...]
        out_ref[3, 0] = total
        for at in (3, 2, 1):
            total = (total.astype(jnp.float32) + dot_nt(b_ref[at], w_ref[at, 0])).astype(
                jnp.bfloat16
            )
            out_ref[at - 1, 0] = total

    return call(
        kernel,
        (steps,),
        [
            pl.BlockSpec((rows, block), lambda i: (0, i)),
            whole((4, rows, head_size)),
            pl.BlockSpec((4, 1, block, head_size), lambda i: (0, i, 0, 0)),
        ],
        pl.BlockSpec((4, 1, rows, block), lambda i: (0, i // 2, 0, i % 2)),
        jax.ShapeDtypeStruct((4, 2, rows, share), jnp.bfloat16),
        cost=pl.CostEstimate(
            flops=6 * rows * head_size * chip_width,
            bytes_accessed=8 * chip_width * head_size,
            transcendentals=0,
        ),
    )(gradient, backs, weights)


def averaged(picked, back, gradient, hidden, contributors):
    rows, share = picked.shape
    head_size = back.shape[1]
    steps = 4
    block = share // steps

    def kernel(count_ref, p_ref, b_ref, g_ref, h_ref, out_ref, sum_ref):
        value = dot(p_ref[...], b_ref[...], ((0,), (0,))) / count_ref[0]
        output = dot(g_ref[...], h_ref[...], ((0,), (0,))) / count_ref[0]
        out_ref[:, :head_size] = value
        out_ref[:, head_size:] = output
        square = jnp.sum(value * value + output * output)

        @pl.when(pl.program_id(0) == 0)
        def _():
            sum_ref[...] = jnp.zeros_like(sum_ref)

        sum_ref[...] += square

    return call(
        kernel,
        (steps,),
        [
            pl.BlockSpec(memory_space=pltpu.SMEM),
            pl.BlockSpec((rows, block), lambda i: (0, i)),
            whole((rows, head_size)),
            pl.BlockSpec((rows, block), lambda i: (0, i)),
            whole((rows, head_size)),
        ],
        [
            pl.BlockSpec((block, 2 * head_size), lambda i: (i, 0)),
            whole((8, 128)),
        ],
        [
            jax.ShapeDtypeStruct((share, 2 * head_size), jnp.float32),
            jax.ShapeDtypeStruct((8, 128), jnp.float32),
        ],
        cost=pl.CostEstimate(
            flops=4 * rows * share * head_size,
            bytes_accessed=4 * rows * (share + head_size) + 8 * share * head_size,
            transcendentals=0,
        ),
    )(contributors, picked, back, gradient, hidden)


def update(factor, grads, master, moment_one, moment_two):
    share, columns = grads.shape
    block = min(share, 128)

    def kernel(factor_ref, grad_ref, master_ref, one_ref, two_ref, out_ref, new_one_ref, new_two_ref):
        scaled = factor_ref[0] * grad_ref[...]
        new_one = beta_one * one_ref[0].astype(jnp.float32) + (1.0 - beta_one) * scaled
        new_two = beta_two * two_ref[0].astype(jnp.float32) + (1.0 - beta_two) * scaled * scaled
        hat_one = new_one / (1.0 - beta_one**step_count)
        hat_two = new_two / (1.0 - beta_two**step_count)
        old_master = master_ref[0]
        out_ref[0] = old_master - learn_rate * (
            hat_one / (jnp.sqrt(hat_two) + adam_eps) + weight_decay * old_master
        )
        new_one_ref[0] = new_one.astype(jnp.bfloat16)
        new_two_ref[0] = new_two.astype(jnp.bfloat16)

    tile = pl.BlockSpec((1, block, columns), lambda i: (0, i, 0))
    return call(
        kernel,
        (share // block,),
        [
            pl.BlockSpec(memory_space=pltpu.SMEM),
            pl.BlockSpec((block, columns), lambda i: (i, 0)),
            tile,
            tile,
            tile,
        ],
        [tile] * 3,
        [
            jax.ShapeDtypeStruct((1, share, columns), jnp.float32),
            jax.ShapeDtypeStruct((1, share, columns), jnp.bfloat16),
            jax.ShapeDtypeStruct((1, share, columns), jnp.bfloat16),
        ],
        cost=pl.CostEstimate(
            flops=20 * share * columns,
            bytes_accessed=20 * share * columns,
            transcendentals=share * columns,
        ),
    )(factor, grads, master, moment_one, moment_two)


def shards(
    acts, out_grad, w_value, w_output, order, alive, flags, clip_rms, master, moment_one, moment_two
):
    z, y, x, core = (lax.axis_index(axis) for axis in ("z", "y", "x", "core"))
    planes, columns, across = (lax.axis_size(axis) for axis in ("z", "y", "x"))
    replicas = across * lax.axis_size("core")
    own_value, own_output = w_value[0], w_output[0]
    share, head_size = own_value.shape
    micro, tok_rows, width = out_grad.shape
    rows = micro * tok_rows
    chip_width = 2 * share

    output_weight = lax.all_gather(own_output, PLANE, axis=0)
    value_weight = lax.all_gather(own_value, PLANE, axis=0)
    flag_row = lax.all_gather(flags[0, 0], DP)

    top = out_grad.reshape(rows, width)
    own_slice = lax.dynamic_slice(top, (0, x * chip_width), (rows, chip_width))
    gradient = jnp.where(
        jnp.logical_and(z == planes - 1, x == y), own_slice, jnp.zeros_like(own_slice)
    )
    for turn in range(1, across):
        other = lax.rem(x + turn, across)
        piece = lax.dynamic_slice(top, (0, other * chip_width), (rows, chip_width))
        base = (planes - 1) * columns * across
        pairs = [
            (base + i * across + i, base + i * across + (i + turn) % across) for i in range(columns)
        ]
        gradient = gradient + lax.ppermute(piece, ("z", "y", "x"), pairs)

    keep = alive * (1 - flag_row)
    replica = lax.axis_index(DP)
    own_keep = (alive[replica] * (1 - flags[0, 0])).astype(jnp.bfloat16)
    picked = jnp.take(acts[0], order[0], axis=0).reshape(rows, width) * own_keep
    picked = lax.all_to_all(picked, DP, split_axis=1, concat_axis=0, tiled=True)
    hidden_part = dot(picked, own_value, ((1,), (0,))).astype(jnp.bfloat16)
    hidden_part = lax.all_to_all(
        hidden_part.reshape(replicas, rows, head_size), DP, split_axis=0, concat_axis=0, tiled=True
    )
    hidden = jnp.sum(hidden_part.astype(jnp.float32), axis=0).astype(jnp.bfloat16)
    output_weight, hidden, gradient, keep = lax.optimization_barrier(
        (output_weight, hidden, gradient, keep)
    )
    hidden = lax.all_gather(hidden, DP, axis=0, tiled=True)

    eighth = head_size // replicas
    at_row = lax.axis_index(PLANE) * eighth
    link = []
    for at, other in PAIRS:
        total = 0.0
        for half in range(2):
            left = lax.dynamic_slice(output_weight[2 * at + half], (at_row, 0), (eighth, share))
            total = total + dot(left, value_weight[2 * other + half], ((1,), (0,)))
        link.append(total.astype(jnp.bfloat16))
    (low, low_got), (high, high_got) = addends_over_x((jnp.stack(link[:3]), jnp.stack(link[3:])))
    link = jnp.concatenate(
        [
            (low.astype(jnp.float32) + low_got.astype(jnp.float32)).astype(jnp.bfloat16),
            (high.astype(jnp.float32) + high_got.astype(jnp.float32)).astype(jnp.bfloat16),
        ]
    )
    links = lax.all_gather(link, PLANE, axis=0)

    kept_gradient, kept_back = gradient, None
    for turn in range(planes):
        high = project(gradient, output_weight, 2)
        low = project(gradient, output_weight, 0)
        addends = addends_over_x((low, high))
        if turn < planes - 1:
            backs, gradient = advance(gradient, addends, links, value_weight)
            gradient = lax.ppermute(gradient, "z", [(i, i - 1) for i in range(1, planes)])
            kept_gradient = kept_gradient + gradient
        else:
            backs = solve_last(addends, links)
        kept_back = backs if kept_back is None else kept_back + backs

    sent = rebuild(kept_gradient, kept_back, value_weight)
    grad_rows = lax.all_to_all(
        sent.reshape(replicas, rows, share), PLANE, split_axis=0, concat_axis=0, tiled=True
    )
    grad_rows = grad_rows.reshape(replicas * rows, share)
    backs = lax.all_to_all(kept_back, "y", split_axis=0, concat_axis=0, tiled=True)
    others = swap(backs, "core", 1)
    back_rows = jnp.stack(
        [jnp.where(core == 0, backs, others), jnp.where(core == 0, others, backs)], axis=1
    ).reshape(replicas * rows, head_size)

    contributors = jnp.maximum(jnp.sum(keep).astype(jnp.float32), 1.0)[None]
    grads, square = averaged(picked, back_rows, grad_rows, hidden, contributors)
    norm = jnp.sqrt(sum_over_all(square)[0, :1])
    sections = planes * columns
    threshold = clip_rms * math.sqrt(2 * width * head_size * sections)
    factor = jnp.minimum(1.0, threshold / (norm + 1e-06))
    return tuple(update(factor, grads, master, moment_one, moment_two))


def solution(mesh):
    physical = Mesh(mesh.devices.reshape(4, 4, 4, 2), ("z", "y", "x", "core"))
    in_specs = (
        P(SECTION, None, DP, None),
        P(None, DP, None),
        P(SECTION, DP, None),
        P(SECTION, None, DP),
        P(DP, None),
        P(),
        P(SECTION, DP),
        P(),
        P(SECTION, DP, None),
        P(SECTION, DP, None),
        P(SECTION, DP, None),
    )
    out_specs = (P(SECTION, DP, None), P(SECTION, DP, None), P(SECTION, DP, None))
    return jax.shard_map(
        shards, mesh=physical, in_specs=in_specs, out_specs=out_specs, check_vma=False
    )
```

```python
import math

import jax
import jax.numpy as jnp
from jax import lax
from jax.experimental import pallas as pl
from jax.experimental.pallas import tpu as pltpu
from jax.sharding import Mesh
from jax.sharding import PartitionSpec as P

beta_one = 0.9
beta_two = 0.95
adam_eps = 1e-08
learn_rate = 0.01
weight_decay = 0.1
step_count = 100

SECTION = ("z", "y")
DP = ("x", "core")
PLANE = ("y", "core")


VMEM_LIMIT = 18 * 1024 * 1024
PAIRS = ((0, 1), (0, 2), (1, 2), (0, 3), (1, 3), (2, 3))


def dot(left, right, dims):
    return lax.dot_general(left, right, (dims, ((), ())), preferred_element_type=jnp.float32)


def dot_nt(left, right):
    return dot(left, right, ((1,), (1,)))


def call(kernel, grid, in_specs, out_specs, out_shape, scratch=(), cost=None):
    return pl.pallas_call(
        kernel,
        grid=grid,
        in_specs=in_specs,
        out_specs=out_specs,
        out_shape=out_shape,
        scratch_shapes=list(scratch),
        cost_estimate=cost,
        compiler_params=pltpu.CompilerParams(vmem_limit_bytes=VMEM_LIMIT),
    )


def whole(shape):
    return pl.BlockSpec(shape, lambda *_: (0,) * len(shape))


def swap(value, axis, mask):
    return lax.ppermute(value, axis, [(i, i ^ mask) for i in range(lax.axis_size(axis))])


def turn_by(value, axis, steps):
    count = lax.axis_size(axis)
    return lax.ppermute(value, axis, [(i, (i + steps) % count) for i in range(count)])


def pack(own_value, own_output):
    share, head_size = own_value.shape
    blocks = share // head_size

    def kernel(v_ref, o_ref, out_ref):
        at = pl.program_id(0)

        @pl.when(at < blocks)
        def _():
            out_ref[0] = v_ref[...]

        @pl.when(at >= blocks)
        def _():
            out_ref[0] = o_ref[...]

    return call(
        kernel,
        (2 * blocks,),
        [
            pl.BlockSpec((head_size, head_size), lambda i: (jnp.minimum(i, blocks - 1), 0)),
            pl.BlockSpec((head_size, head_size), lambda i: (0, jnp.maximum(i - blocks, 0))),
        ],
        pl.BlockSpec((1, head_size, head_size), lambda i: (i, 0, 0)),
        jax.ShapeDtypeStruct((2 * blocks, head_size, head_size), jnp.bfloat16),
        cost=pl.CostEstimate(
            flops=0, bytes_accessed=8 * share * head_size, transcendentals=0
        ),
    )(own_value, own_output)


def link_parts(stack, place):
    columns, cores, double, head_size, _ = stack.shape
    blocks = double // 2
    eighth = head_size // (columns * cores)
    total = len(PAIRS)
    table = jnp.array([pair[0] for pair in PAIRS] + [pair[1] for pair in PAIRS], jnp.int32)
    table = jnp.concatenate([table, place[None].astype(jnp.int32)])

    def kernel(table_ref, o_ref, v_ref, out_ref):
        part = 0.0
        for side in range(cores):
            for k in range(blocks):
                part = part + dot(o_ref[0, side, k], v_ref[0, side, k], ((1,), (0,)))
        out_ref[0] = part.astype(jnp.bfloat16)

    return pl.pallas_call(
        kernel,
        grid_spec=pltpu.PrefetchScalarGridSpec(
            num_scalar_prefetch=1,
            grid=(total,),
            in_specs=[
                pl.BlockSpec(
                    (1, cores, blocks, eighth, head_size),
                    lambda i, table: (table[i], 0, 1, table[2 * total], 0),
                ),
                pl.BlockSpec(
                    (1, cores, blocks, head_size, head_size),
                    lambda i, table: (table[total + i], 0, 0, 0, 0),
                ),
            ],
            out_specs=pl.BlockSpec((1, eighth, head_size), lambda i, table: (i, 0, 0)),
        ),
        out_shape=jax.ShapeDtypeStruct((total, eighth, head_size), jnp.bfloat16),
        cost_estimate=pl.CostEstimate(
            flops=4 * total * eighth * blocks * head_size * head_size,
            bytes_accessed=12 * blocks * head_size * head_size,
            transcendentals=0,
        ),
        compiler_params=pltpu.CompilerParams(vmem_limit_bytes=VMEM_LIMIT),
    )(table, stack, stack)


def addends_over_x(parts, masks=((1, 3), (3, 1))):
    pairs = []
    firsts = [swap(part, "x", masks[i][0]) for i, part in enumerate(parts)]
    halves = [
        (part.astype(jnp.float32) + other.astype(jnp.float32)).astype(jnp.bfloat16)
        for part, other in zip(parts, firsts)
    ]
    for i, half in enumerate(halves):
        pairs.append((half, swap(half, "x", masks[i][1])))
    return pairs


def sum_over_all(value):
    value = value + swap(value, "core", 1)
    for axis in ("x", "y", "z"):
        got = [turn_by(value, axis, steps) for steps in (1, 3, 2)]
        value = value + got[0] + got[1] + got[2]
    return value


def project(gradient, stack, first):
    rows, chip_width = gradient.shape
    columns, cores, double, head_size, _ = stack.shape
    blocks = double // 2

    def kernel(g_ref, w_ref, out_ref):
        part = 0.0
        for side in range(cores):
            for k in range(blocks):
                start = (side * blocks + k) * head_size
                part = part + dot_nt(g_ref[:, start : start + head_size], w_ref[0, side, k])
        out_ref[...] = part.astype(jnp.bfloat16)

    return call(
        kernel,
        (2,),
        [
            whole((rows, chip_width)),
            pl.BlockSpec(
                (1, cores, blocks, head_size, head_size), lambda i: (first + i, 0, 1, 0, 0)
            ),
        ],
        pl.BlockSpec((rows, head_size), lambda i: (0, i)),
        jax.ShapeDtypeStruct((rows, 2 * head_size), jnp.bfloat16),
        cost=pl.CostEstimate(
            flops=4 * rows * chip_width * head_size,
            bytes_accessed=4 * chip_width * head_size,
            transcendentals=0,
        ),
    )(gradient, stack)


def solve(addends, links, b_ref):
    low, low_got, high, high_got = addends
    head_size = links.shape[-1]
    sums = []
    for own, got in ((low, low_got), (high, high_got)):
        both = own[...].astype(jnp.float32) + got[...].astype(jnp.float32)
        sums += [both[:, :head_size], both[:, head_size:]]
    backs = [None] * 4
    for at in (3, 2, 1, 0):
        total = sums[at]
        for other in range(at + 1, 4):
            link = links[:, PAIRS.index((at, other))].reshape(head_size, head_size)
            total = total + dot_nt(backs[other], link)
        backs[at] = total.astype(jnp.bfloat16)
        b_ref[at] = backs[at]


def advance(gradient, addends, links, weights):
    rows, chip_width = gradient.shape
    _, cores, double, head_size, _ = weights.shape
    blocks = double // 2
    steps = cores * blocks
    block = head_size
    flat = [array for pair in addends for array in pair]

    def kernel(g_ref, low, low_got, high, high_got, m_ref, w_ref, b_ref, out_ref):
        @pl.when(pl.program_id(0) == 0)
        def _():
            solve((low, low_got, high, high_got), m_ref, b_ref)

        total = g_ref[...].astype(jnp.float32)
        for at in range(4):
            total = total + dot_nt(b_ref[at], w_ref[at, 0, 0])
        out_ref[...] = total.astype(jnp.bfloat16)

    return call(
        kernel,
        (steps,),
        [pl.BlockSpec((rows, block), lambda i: (0, i))]
        + [whole((rows, 2 * head_size))] * 4
        + [
            whole(links.shape),
            pl.BlockSpec(
                (4, 1, 1, block, head_size), lambda i: (0, i // blocks, i % blocks, 0, 0)
            ),
        ],
        [
            whole((4, rows, head_size)),
            pl.BlockSpec((rows, block), lambda i: (0, i)),
        ],
        [
            jax.ShapeDtypeStruct((4, rows, head_size), jnp.bfloat16),
            jax.ShapeDtypeStruct((rows, chip_width), jnp.bfloat16),
        ],
        cost=pl.CostEstimate(
            flops=2 * rows * head_size * (6 * head_size + 4 * chip_width),
            bytes_accessed=8 * chip_width * head_size + 12 * head_size * head_size,
            transcendentals=0,
        ),
    )(gradient, *flat, links, weights)


def solve_last(addends, links):
    rows, two = addends[0][0].shape
    head_size = two // 2
    flat = [array for pair in addends for array in pair]

    def kernel(low, low_got, high, high_got, m_ref, b_ref):
        solve((low, low_got, high, high_got), m_ref, b_ref)

    return call(
        kernel,
        (1,),
        [whole((rows, two))] * 4 + [whole(links.shape)],
        whole((4, rows, head_size)),
        jax.ShapeDtypeStruct((4, rows, head_size), jnp.bfloat16),
        cost=pl.CostEstimate(
            flops=12 * rows * head_size * head_size,
            bytes_accessed=12 * head_size * head_size,
            transcendentals=0,
        ),
    )(*flat, links)


def rebuild(gradient, backs, weights):
    rows, chip_width = gradient.shape
    _, cores, double, head_size, _ = weights.shape
    blocks = double // 2

    def kernel(g_ref, b_ref, w_ref, out_ref):
        at_block = pl.program_id(1)

        @pl.when(at_block < blocks)
        def _():
            total = g_ref[...]
            out_ref[3, 0] = total
            for at in (3, 2, 1):
                total = (total.astype(jnp.float32) + dot_nt(b_ref[at], w_ref[at, 0, 0])).astype(
                    jnp.bfloat16
                )
                out_ref[at - 1, 0] = total

        @pl.when(at_block == blocks)
        def _():
            for at in range(4):
                out_ref[at, 0] = b_ref[at]

    def inner(k):
        return jnp.minimum(k, blocks - 1)

    return call(
        kernel,
        (cores, blocks + 1),
        [
            pl.BlockSpec((rows, head_size), lambda i, k: (0, i * blocks + inner(k))),
            whole((4, rows, head_size)),
            pl.BlockSpec(
                (4, 1, 1, head_size, head_size), lambda i, k: (0, i, inner(k), 0, 0)
            ),
        ],
        pl.BlockSpec((4, 1, rows, head_size), lambda i, k: (0, i, 0, k)),
        jax.ShapeDtypeStruct((4, cores, rows, chip_width // cores + head_size), jnp.bfloat16),
        cost=pl.CostEstimate(
            flops=6 * rows * head_size * chip_width,
            bytes_accessed=8 * chip_width * head_size,
            transcendentals=0,
        ),
    )(gradient, backs, weights)


def averaged(picked, got, hidden, contributors):
    rows, share = picked.shape
    head_size = hidden.shape[1]
    steps = 4
    block = share // steps

    def kernel(count_ref, p_ref, b_ref, g_ref, h_ref, out_ref, sum_ref):
        value = dot(p_ref[...], b_ref[...], ((0,), (0,))) / count_ref[0]
        output = dot(g_ref[...], h_ref[...], ((0,), (0,))) / count_ref[0]
        out_ref[:, :head_size] = value
        out_ref[:, head_size:] = output
        square = jnp.sum(value * value + output * output)

        @pl.when(pl.program_id(0) == 0)
        def _():
            sum_ref[...] = jnp.zeros_like(sum_ref)

        sum_ref[...] += square

    return call(
        kernel,
        (steps,),
        [
            pl.BlockSpec(memory_space=pltpu.SMEM),
            pl.BlockSpec((rows, block), lambda i: (0, i)),
            pl.BlockSpec((rows, head_size), lambda i: (0, share // head_size)),
            pl.BlockSpec((rows, block), lambda i: (0, i)),
            whole((rows, head_size)),
        ],
        [
            pl.BlockSpec((block, 2 * head_size), lambda i: (i, 0)),
            whole((8, 128)),
        ],
        [
            jax.ShapeDtypeStruct((share, 2 * head_size), jnp.float32),
            jax.ShapeDtypeStruct((8, 128), jnp.float32),
        ],
        cost=pl.CostEstimate(
            flops=4 * rows * share * head_size,
            bytes_accessed=4 * rows * (share + head_size) + 8 * share * head_size,
            transcendentals=0,
        ),
    )(contributors, picked, got, got, hidden)


def update(factor, grads, master, moment_one, moment_two):
    share, columns = grads.shape
    block = min(share, 128)

    def kernel(factor_ref, grad_ref, master_ref, one_ref, two_ref, out_ref, new_one_ref, new_two_ref):
        scaled = factor_ref[0] * grad_ref[...]
        new_one = beta_one * one_ref[0].astype(jnp.float32) + (1.0 - beta_one) * scaled
        new_two = beta_two * two_ref[0].astype(jnp.float32) + (1.0 - beta_two) * scaled * scaled
        hat_one = new_one / (1.0 - beta_one**step_count)
        hat_two = new_two / (1.0 - beta_two**step_count)
        old_master = master_ref[0]
        out_ref[0] = old_master - learn_rate * (
            hat_one / (jnp.sqrt(hat_two) + adam_eps) + weight_decay * old_master
        )
        new_one_ref[0] = new_one.astype(jnp.bfloat16)
        new_two_ref[0] = new_two.astype(jnp.bfloat16)

    tile = pl.BlockSpec((1, block, columns), lambda i: (0, i, 0))
    return call(
        kernel,
        (share // block,),
        [
            pl.BlockSpec(memory_space=pltpu.SMEM),
            pl.BlockSpec((block, columns), lambda i: (i, 0)),
            tile,
            tile,
            tile,
        ],
        [tile] * 3,
        [
            jax.ShapeDtypeStruct((1, share, columns), jnp.float32),
            jax.ShapeDtypeStruct((1, share, columns), jnp.bfloat16),
            jax.ShapeDtypeStruct((1, share, columns), jnp.bfloat16),
        ],
        cost=pl.CostEstimate(
            flops=20 * share * columns,
            bytes_accessed=20 * share * columns,
            transcendentals=share * columns,
        ),
    )(factor, grads, master, moment_one, moment_two)


def shards(
    acts, out_grad, w_value, w_output, order, alive, flags, clip_rms, master, moment_one, moment_two
):
    z, y, x, core = (lax.axis_index(axis) for axis in ("z", "y", "x", "core"))
    planes, columns, across = (lax.axis_size(axis) for axis in ("z", "y", "x"))
    replicas = across * lax.axis_size("core")
    own_value, own_output = w_value[0], w_output[0]
    share, head_size = own_value.shape
    micro, tok_rows, width = out_grad.shape
    rows = micro * tok_rows
    chip_width = 2 * share

    bundle = pack(own_value, own_output)
    stack = lax.all_gather(bundle, PLANE, axis=0).reshape((columns, 2) + bundle.shape)

    top = out_grad.reshape(rows, width)
    piece = lax.dynamic_slice(top, (0, z * chip_width), (rows, chip_width))
    base = (planes - 1) * columns * across
    pairs = [
        ((j * columns + i) * across + i, base + i * across + j)
        for i in range(columns)
        for j in range(across)
    ]
    gradient = lax.ppermute(piece, ("z", "y", "x"), pairs)

    replica = lax.axis_index(DP)
    keep = (alive[replica] * (1 - flags[0, 0])).astype(jnp.float32)
    count = jnp.full((8, 128), keep)
    count = count + swap(count, "core", 1)
    count = count + sum(turn_by(count, "x", steps) for steps in range(1, across))
    picked = jnp.take(acts[0], order[0], axis=0).reshape(rows, width) * keep.astype(jnp.bfloat16)
    picked = lax.all_to_all(picked, DP, split_axis=1, concat_axis=0, tiled=True)

    hidden_part = dot(picked, own_value, ((1,), (0,))).astype(jnp.bfloat16)
    hidden_part = lax.all_to_all(
        hidden_part.reshape(replicas, rows, head_size), DP, split_axis=0, concat_axis=0, tiled=True
    )

    hidden = jnp.sum(hidden_part.astype(jnp.float32), axis=0).astype(jnp.bfloat16)
    stack, hidden, gradient, count = lax.optimization_barrier((stack, hidden, gradient, count))
    hidden = lax.all_gather(hidden, DP, axis=0, tiled=True)

    link = link_parts(stack, lax.axis_index(PLANE))
    (low, low_got), (high, high_got) = addends_over_x((link[:3], link[3:]))
    link = jnp.concatenate(
        [
            (low.astype(jnp.float32) + low_got.astype(jnp.float32)).astype(jnp.bfloat16),
            (high.astype(jnp.float32) + high_got.astype(jnp.float32)).astype(jnp.bfloat16),
        ]
    )
    links = lax.all_gather(link, PLANE, axis=0)

    kept_gradient, kept_back = gradient, None
    for turn in range(planes):
        high = project(gradient, stack, 2)
        low = project(gradient, stack, 0)
        addends = addends_over_x((low, high))
        if turn < planes - 1:
            backs, gradient = advance(gradient, addends, links, stack)
            gradient = lax.ppermute(gradient, "z", [(i, i - 1) for i in range(1, planes)])
            kept_gradient = kept_gradient + gradient
        else:
            backs = solve_last(addends, links)
        kept_back = backs if kept_back is None else kept_back + backs

    sent = rebuild(kept_gradient, kept_back, stack)
    got = lax.all_to_all(
        sent.reshape(replicas, rows, share + head_size), PLANE, split_axis=0, concat_axis=0, tiled=True
    ).reshape(replicas * rows, share + head_size)

    contributors = jnp.maximum(count[0, :1], 1.0)
    grads, square = averaged(picked, got, hidden, contributors)
    norm = jnp.sqrt(sum_over_all(square)[0, :1])
    sections = planes * columns
    threshold = clip_rms * math.sqrt(2 * width * head_size * sections)
    factor = jnp.minimum(1.0, threshold / (norm + 1e-06))
    return tuple(update(factor, grads, master, moment_one, moment_two))


def solution(mesh):
    physical = Mesh(mesh.devices.reshape(4, 4, 4, 2), ("z", "y", "x", "core"))
    in_specs = (
        P(SECTION, None, DP, None),
        P(None, DP, None),
        P(SECTION, DP, None),
        P(SECTION, None, DP),
        P(DP, None),
        P(),
        P(SECTION, DP),
        P(),
        P(SECTION, DP, None),
        P(SECTION, DP, None),
        P(SECTION, DP, None),
    )
    out_specs = (P(SECTION, DP, None), P(SECTION, DP, None), P(SECTION, DP, None))
    return jax.shard_map(
        shards, mesh=physical, in_specs=in_specs, out_specs=out_specs, check_vma=False
    )
```

```python
import math

import jax
import jax.numpy as jnp
from jax import lax
from jax.experimental import pallas as pl
from jax.experimental.pallas import tpu as pltpu
from jax.sharding import Mesh
from jax.sharding import PartitionSpec as P

beta_one = 0.9
beta_two = 0.95
adam_eps = 1e-08
learn_rate = 0.01
weight_decay = 0.1
step_count = 100

SECTION = ("z", "y")
DP = ("x", "core")
PLANE = ("y", "core")


VMEM_LIMIT = 18 * 1024 * 1024
STREAM_LIMIT = 60 * 1024 * 1024
PAIRS = ((0, 1), (0, 2), (1, 2), (0, 3), (1, 3), (2, 3))


def dot(left, right, dims):
    return lax.dot_general(left, right, (dims, ((), ())), preferred_element_type=jnp.float32)


def dot_nt(left, right):
    return dot(left, right, ((1,), (1,)))


def call(kernel, grid, in_specs, out_specs, out_shape, scratch=(), cost=None, limit=VMEM_LIMIT):
    return pl.pallas_call(
        kernel,
        grid=grid,
        in_specs=in_specs,
        out_specs=out_specs,
        out_shape=out_shape,
        scratch_shapes=list(scratch),
        cost_estimate=cost,
        compiler_params=pltpu.CompilerParams(vmem_limit_bytes=limit),
    )


def whole(shape):
    return pl.BlockSpec(shape, lambda *_: (0,) * len(shape))


def swap(value, axis, mask):
    return lax.ppermute(value, axis, [(i, i ^ mask) for i in range(lax.axis_size(axis))])


def turn_by(value, axis, steps):
    count = lax.axis_size(axis)
    return lax.ppermute(value, axis, [(i, (i + steps) % count) for i in range(count)])


def pack(own_value, own_output):
    share, head_size = own_value.shape
    blocks = share // head_size

    def kernel(v_ref, o_ref, out_ref):
        at = pl.program_id(0)

        @pl.when(at < blocks)
        def _():
            out_ref[0] = v_ref[...]

        @pl.when(at >= blocks)
        def _():
            out_ref[0] = o_ref[...]

    return call(
        kernel,
        (2 * blocks,),
        [
            pl.BlockSpec((head_size, head_size), lambda i: (jnp.minimum(i, blocks - 1), 0)),
            pl.BlockSpec((head_size, head_size), lambda i: (0, jnp.maximum(i - blocks, 0))),
        ],
        pl.BlockSpec((1, head_size, head_size), lambda i: (i, 0, 0)),
        jax.ShapeDtypeStruct((2 * blocks, head_size, head_size), jnp.bfloat16),
        cost=pl.CostEstimate(
            flops=0, bytes_accessed=8 * share * head_size, transcendentals=0
        ),
    )(own_value, own_output)


def link_parts(stack, place):
    columns, cores, double, head_size, _ = stack.shape
    blocks = double // 2
    eighth = head_size // (columns * cores)
    total = len(PAIRS)
    table = jnp.array([pair[0] for pair in PAIRS] + [pair[1] for pair in PAIRS], jnp.int32)
    table = jnp.concatenate([table, place[None].astype(jnp.int32)])

    def kernel(table_ref, o_ref, v_ref, out_ref):
        part = 0.0
        for side in range(cores):
            for k in range(blocks):
                part = part + dot(o_ref[0, side, k], v_ref[0, side, k], ((1,), (0,)))
        out_ref[0] = part.astype(jnp.bfloat16)

    return pl.pallas_call(
        kernel,
        grid_spec=pltpu.PrefetchScalarGridSpec(
            num_scalar_prefetch=1,
            grid=(total,),
            in_specs=[
                pl.BlockSpec(
                    (1, cores, blocks, eighth, head_size),
                    lambda i, table: (table[i], 0, 1, table[2 * total], 0),
                ),
                pl.BlockSpec(
                    (1, cores, blocks, head_size, head_size),
                    lambda i, table: (table[total + i], 0, 0, 0, 0),
                ),
            ],
            out_specs=pl.BlockSpec((1, eighth, head_size), lambda i, table: (i, 0, 0)),
        ),
        out_shape=jax.ShapeDtypeStruct((total, eighth, head_size), jnp.bfloat16),
        cost_estimate=pl.CostEstimate(
            flops=4 * total * eighth * blocks * head_size * head_size,
            bytes_accessed=12 * blocks * head_size * head_size,
            transcendentals=0,
        ),
        compiler_params=pltpu.CompilerParams(vmem_limit_bytes=STREAM_LIMIT),
    )(table, stack, stack)


def addends_over_x(parts, masks=((1, 3), (3, 1))):
    pairs = []
    firsts = [swap(part, "x", masks[i][0]) for i, part in enumerate(parts)]
    halves = [
        (part.astype(jnp.float32) + other.astype(jnp.float32)).astype(jnp.bfloat16)
        for part, other in zip(parts, firsts)
    ]
    for i, half in enumerate(halves):
        pairs.append((half, swap(half, "x", masks[i][1])))
    return pairs


def sum_over_all(value):
    value = value + swap(value, "core", 1)
    for axis in ("x", "y", "z"):
        got = [turn_by(value, axis, steps) for steps in (1, 3, 2)]
        value = value + got[0] + got[1] + got[2]
    return value


def project(gradient, stack, first):
    rows, chip_width = gradient.shape
    columns, cores, double, head_size, _ = stack.shape
    blocks = double // 2

    def kernel(g_ref, w_ref, out_ref):
        part = 0.0
        for side in range(cores):
            for k in range(blocks):
                start = (side * blocks + k) * head_size
                part = part + dot_nt(g_ref[:, start : start + head_size], w_ref[0, side, k])
        out_ref[...] = part.astype(jnp.bfloat16)

    return call(
        kernel,
        (2,),
        [
            whole((rows, chip_width)),
            pl.BlockSpec(
                (1, cores, blocks, head_size, head_size), lambda i: (first + i, 0, 1, 0, 0)
            ),
        ],
        pl.BlockSpec((rows, head_size), lambda i: (0, i)),
        jax.ShapeDtypeStruct((rows, 2 * head_size), jnp.bfloat16),
        cost=pl.CostEstimate(
            flops=4 * rows * chip_width * head_size,
            bytes_accessed=4 * chip_width * head_size,
            transcendentals=0,
        ),
    )(gradient, stack)


def solve(addends, links, b_ref):
    low, low_got, high, high_got = addends
    head_size = links.shape[-1]
    sums = []
    for own, got in ((low, low_got), (high, high_got)):
        both = own[...].astype(jnp.float32) + got[...].astype(jnp.float32)
        sums += [both[:, :head_size], both[:, head_size:]]
    backs = [None] * 4
    for at in (3, 2, 1, 0):
        total = sums[at]
        for other in range(at + 1, 4):
            link = links[:, PAIRS.index((at, other))].reshape(head_size, head_size)
            total = total + dot_nt(backs[other], link)
        backs[at] = total.astype(jnp.bfloat16)
        b_ref[at] = backs[at]


def advance(gradient, addends, links, weights, ready=(), limit=VMEM_LIMIT):
    rows, chip_width = gradient.shape
    _, cores, double, head_size, _ = weights.shape
    blocks = double // 2
    steps = cores * blocks
    block = head_size
    flat = [array for pair in addends for array in pair]

    def kernel(g_ref, low, low_got, high, high_got, m_ref, w_ref, *others):
        b_ref, out_ref = others[-2:]

        @pl.when(pl.program_id(0) == 0)
        def _():
            solve((low, low_got, high, high_got), m_ref, b_ref)

        total = g_ref[...].astype(jnp.float32)
        for at in range(4):
            total = total + dot_nt(b_ref[at], w_ref[at, 0, 0])
        out_ref[...] = total.astype(jnp.bfloat16)

    return call(
        kernel,
        (steps,),
        [pl.BlockSpec((rows, block), lambda i: (0, i))]
        + [whole((rows, 2 * head_size))] * 4
        + [
            whole(links.shape),
            pl.BlockSpec(
                (4, 1, 1, block, head_size), lambda i: (0, i // blocks, i % blocks, 0, 0)
            ),
        ]
        + [pl.BlockSpec(memory_space=pl.ANY)] * len(ready),
        [
            whole((4, rows, head_size)),
            pl.BlockSpec((rows, block), lambda i: (0, i)),
        ],
        [
            jax.ShapeDtypeStruct((4, rows, head_size), jnp.bfloat16),
            jax.ShapeDtypeStruct((rows, chip_width), jnp.bfloat16),
        ],
        cost=pl.CostEstimate(
            flops=2 * rows * head_size * (6 * head_size + 4 * chip_width),
            bytes_accessed=8 * chip_width * head_size + 12 * head_size * head_size,
            transcendentals=0,
        ),
        limit=limit,
    )(gradient, *flat, links, weights, *ready)


def solve_last(addends, links):
    rows, two = addends[0][0].shape
    head_size = two // 2
    flat = [array for pair in addends for array in pair]

    def kernel(low, low_got, high, high_got, m_ref, b_ref):
        solve((low, low_got, high, high_got), m_ref, b_ref)

    return call(
        kernel,
        (1,),
        [whole((rows, two))] * 4 + [whole(links.shape)],
        whole((4, rows, head_size)),
        jax.ShapeDtypeStruct((4, rows, head_size), jnp.bfloat16),
        cost=pl.CostEstimate(
            flops=12 * rows * head_size * head_size,
            bytes_accessed=12 * head_size * head_size,
            transcendentals=0,
        ),
    )(*flat, links)


def rebuild(gradient, backs, weights):
    rows, chip_width = gradient.shape
    _, cores, double, head_size, _ = weights.shape
    blocks = double // 2

    def kernel(g_ref, b_ref, w_ref, out_ref):
        at_block = pl.program_id(1)

        @pl.when(at_block < blocks)
        def _():
            total = g_ref[...]
            out_ref[3, 0] = total
            for at in (3, 2, 1):
                total = (total.astype(jnp.float32) + dot_nt(b_ref[at], w_ref[at, 0, 0])).astype(
                    jnp.bfloat16
                )
                out_ref[at - 1, 0] = total

        @pl.when(at_block == blocks)
        def _():
            for at in range(4):
                out_ref[at, 0] = b_ref[at]

    def inner(k):
        return jnp.minimum(k, blocks - 1)

    return call(
        kernel,
        (cores, blocks + 1),
        [
            pl.BlockSpec((rows, head_size), lambda i, k: (0, i * blocks + inner(k))),
            whole((4, rows, head_size)),
            pl.BlockSpec(
                (4, 1, 1, head_size, head_size), lambda i, k: (0, i, inner(k), 0, 0)
            ),
        ],
        pl.BlockSpec((4, 1, rows, head_size), lambda i, k: (0, i, 0, k)),
        jax.ShapeDtypeStruct((4, cores, rows, chip_width // cores + head_size), jnp.bfloat16),
        cost=pl.CostEstimate(
            flops=6 * rows * head_size * chip_width,
            bytes_accessed=8 * chip_width * head_size,
            transcendentals=0,
        ),
    )(gradient, backs, weights)


def averaged(picked, got, hidden, contributors):
    rows, share = picked.shape
    head_size = hidden.shape[1]
    steps = 4
    block = share // steps

    def kernel(count_ref, p_ref, b_ref, g_ref, h_ref, out_ref, sum_ref):
        value = dot(p_ref[...], b_ref[...], ((0,), (0,))) / count_ref[0]
        output = dot(g_ref[...], h_ref[...], ((0,), (0,))) / count_ref[0]
        out_ref[:, :head_size] = value
        out_ref[:, head_size:] = output
        square = jnp.sum(value * value + output * output)

        @pl.when(pl.program_id(0) == 0)
        def _():
            sum_ref[...] = jnp.zeros_like(sum_ref)

        sum_ref[...] += square

    return call(
        kernel,
        (steps,),
        [
            pl.BlockSpec(memory_space=pltpu.SMEM),
            pl.BlockSpec((rows, block), lambda i: (0, i)),
            pl.BlockSpec((rows, head_size), lambda i: (0, share // head_size)),
            pl.BlockSpec((rows, block), lambda i: (0, i)),
            whole((rows, head_size)),
        ],
        [
            pl.BlockSpec((block, 2 * head_size), lambda i: (i, 0)),
            whole((8, 128)),
        ],
        [
            jax.ShapeDtypeStruct((share, 2 * head_size), jnp.float32),
            jax.ShapeDtypeStruct((8, 128), jnp.float32),
        ],
        cost=pl.CostEstimate(
            flops=4 * rows * share * head_size,
            bytes_accessed=4 * rows * (share + head_size) + 8 * share * head_size,
            transcendentals=0,
        ),
    )(contributors, picked, got, got, hidden)


def update(factor, grads, master, moment_one, moment_two):
    share, columns = grads.shape
    block = min(share, 128)

    def kernel(factor_ref, grad_ref, master_ref, one_ref, two_ref, out_ref, new_one_ref, new_two_ref):
        scaled = factor_ref[0] * grad_ref[...]
        new_one = beta_one * one_ref[0].astype(jnp.float32) + (1.0 - beta_one) * scaled
        new_two = beta_two * two_ref[0].astype(jnp.float32) + (1.0 - beta_two) * scaled * scaled
        hat_one = new_one / (1.0 - beta_one**step_count)
        hat_two = new_two / (1.0 - beta_two**step_count)
        old_master = master_ref[0]
        out_ref[0] = old_master - learn_rate * (
            hat_one / (jnp.sqrt(hat_two) + adam_eps) + weight_decay * old_master
        )
        new_one_ref[0] = new_one.astype(jnp.bfloat16)
        new_two_ref[0] = new_two.astype(jnp.bfloat16)

    tile = pl.BlockSpec((1, block, columns), lambda i: (0, i, 0))
    return call(
        kernel,
        (share // block,),
        [
            pl.BlockSpec(memory_space=pltpu.SMEM),
            pl.BlockSpec((block, columns), lambda i: (i, 0)),
            tile,
            tile,
            tile,
        ],
        [tile] * 3,
        [
            jax.ShapeDtypeStruct((1, share, columns), jnp.float32),
            jax.ShapeDtypeStruct((1, share, columns), jnp.bfloat16),
            jax.ShapeDtypeStruct((1, share, columns), jnp.bfloat16),
        ],
        cost=pl.CostEstimate(
            flops=20 * share * columns,
            bytes_accessed=20 * share * columns,
            transcendentals=share * columns,
        ),
    )(factor, grads, master, moment_one, moment_two)


def shards(
    acts, out_grad, w_value, w_output, order, alive, flags, clip_rms, master, moment_one, moment_two
):
    z, y, x, core = (lax.axis_index(axis) for axis in ("z", "y", "x", "core"))
    planes, columns, across = (lax.axis_size(axis) for axis in ("z", "y", "x"))
    replicas = across * lax.axis_size("core")
    own_value, own_output = w_value[0], w_output[0]
    share, head_size = own_value.shape
    micro, tok_rows, width = out_grad.shape
    rows = micro * tok_rows
    chip_width = 2 * share

    bundle = pack(own_value, own_output)
    stack = lax.all_gather(bundle, PLANE, axis=0).reshape((columns, 2) + bundle.shape)

    top = out_grad.reshape(rows, width)
    piece = lax.dynamic_slice(top, (0, z * chip_width), (rows, chip_width))
    base = (planes - 1) * columns * across
    pairs = [
        ((j * columns + i) * across + i, base + i * across + j)
        for i in range(columns)
        for j in range(across)
    ]
    gradient = lax.ppermute(piece, ("z", "y", "x"), pairs)

    replica = lax.axis_index(DP)
    keep = (alive[replica] * (1 - flags[0, 0])).astype(jnp.float32)
    count = jnp.full((8, 128), keep)
    count = count + swap(count, "core", 1)
    count = count + sum(turn_by(count, "x", steps) for steps in range(1, across))
    picked = jnp.take(acts[0], order[0], axis=0).reshape(rows, width) * keep.astype(jnp.bfloat16)
    picked = lax.all_to_all(picked, DP, split_axis=1, concat_axis=0, tiled=True)

    hidden_part = dot(picked, own_value, ((1,), (0,))).astype(jnp.bfloat16)
    hidden_part = lax.all_to_all(
        hidden_part.reshape(replicas, rows, head_size), DP, split_axis=0, concat_axis=0, tiled=True
    )

    hidden = jnp.sum(hidden_part.astype(jnp.float32), axis=0).astype(jnp.bfloat16)
    stack, hidden, gradient, count = lax.optimization_barrier((stack, hidden, gradient, count))
    hidden = lax.all_gather(hidden, DP, axis=0, tiled=True)

    link = link_parts(stack, lax.axis_index(PLANE))
    (low, low_got), (high, high_got) = addends_over_x((link[:3], link[3:]))
    link = jnp.concatenate(
        [
            (low.astype(jnp.float32) + low_got.astype(jnp.float32)).astype(jnp.bfloat16),
            (high.astype(jnp.float32) + high_got.astype(jnp.float32)).astype(jnp.bfloat16),
        ]
    )
    links = lax.all_gather(link, PLANE, axis=0)

    kept_gradient, kept_back = gradient, None
    for turn in range(planes):
        high = project(gradient, stack, 2)
        low = project(gradient, stack, 0)
        addends = addends_over_x((low, high))
        if turn < planes - 1:
            ready = (hidden,) if turn == planes - 2 else ()
            limit = STREAM_LIMIT if turn == 0 else VMEM_LIMIT
            backs, gradient = advance(gradient, addends, links, stack, ready, limit)
            gradient = lax.ppermute(gradient, "z", [(i, i - 1) for i in range(1, planes)])
            kept_gradient = kept_gradient + gradient
        else:
            backs = solve_last(addends, links)
        kept_back = backs if kept_back is None else kept_back + backs

    sent = rebuild(kept_gradient, kept_back, stack)
    got = lax.all_to_all(
        sent.reshape(replicas, rows, share + head_size), PLANE, split_axis=0, concat_axis=0, tiled=True
    ).reshape(replicas * rows, share + head_size)

    contributors = jnp.maximum(count[0, :1], 1.0)
    grads, square = averaged(picked, got, hidden, contributors)
    norm = jnp.sqrt(sum_over_all(square)[0, :1])
    sections = planes * columns
    threshold = clip_rms * math.sqrt(2 * width * head_size * sections)
    factor = jnp.minimum(1.0, threshold / (norm + 1e-06))
    return tuple(update(factor, grads, master, moment_one, moment_two))


def solution(mesh):
    physical = Mesh(mesh.devices.reshape(4, 4, 4, 2), ("z", "y", "x", "core"))
    in_specs = (
        P(SECTION, None, DP, None),
        P(None, DP, None),
        P(SECTION, DP, None),
        P(SECTION, None, DP),
        P(DP, None),
        P(),
        P(SECTION, DP),
        P(),
        P(SECTION, DP, None),
        P(SECTION, DP, None),
        P(SECTION, DP, None),
    )
    out_specs = (P(SECTION, DP, None), P(SECTION, DP, None), P(SECTION, DP, None))
    return jax.shard_map(
        shards, mesh=physical, in_specs=in_specs, out_specs=out_specs, check_vma=False
    )
```
